256 devices in a mesh: dp: 8 (over y, z_lo), fsdp: 32 (over z_hi, x, core).
Axes of the slice: x: 4, y: 4, z: 8 (z_hi: 4, z_lo: 2; z = z_hi * 2 + z_lo), core: 2. Of those that a mesh axis runs over, the one named last changes fastest.
Arguments:
- tokens: bfloat16 [49152, 5120], P(('dp', 'fsdp')), may hold values from -6 to 6
- weight: bfloat16 [5120, 2560], P('fsdp'), may hold values from -0.078125 to 0.078125
- norm_gain: float32 [2560], replicated, may hold values from 0.1 to 1.9
- cotangent: bfloat16 [49152, 2560], P(('dp', 'fsdp')), may hold values from -6 to 6
- subspace: bfloat16 [2560, 512], replicated, may hold values from -0.125 to 0.125
- moment: float32 [5120, 512], P('fsdp'), may hold values from -6 to 6
- second: float32 [5120, 512], P('fsdp'), may hold values from 0.05 to 2
Outputs:
- normed: bfloat16 [49152, 2560], P(('dp', 'fsdp'))
- in_grad: bfloat16 [49152, 5120], P(('dp', 'fsdp'))
- moment_new: float32 [5120, 512], P('fsdp')
- second_new: float32 [5120, 512], P('fsdp')
- update: float32 [5120, 2560], P('fsdp')
The draws below stay inside these ranges and needn't reach their ends.
All inputs are finite; a program needn't handle non-finite values.
Results may differ from the reference program's by a relative error of at most 0.008.
Values may be sent and summed in bfloat16 or wider, within the bound.
No kernel may reach another device: no remote copies, remote signals or barrier semaphores. Data moves between devices by JAX's collectives and lax.ppermute only.
A program may use at most 128 MiB of HBM per device.

```python
import math
import jax
import jax.numpy as jnp
from jax import lax

D = 5120
QW = 2560
RANK = 512
TOK_DEV = 192
TOKENS = 49152
N_DP = 8
N_FSDP = 32


def block_scale(rng, shape, cuts, low, largest):
    loudness = 1.0
    for axis_at, blocks in cuts:
        draws = jax.random.uniform(jax.random.fold_in(jax.random.fold_in(rng, 6), axis_at), (blocks,), jnp.float32, low / len(cuts), largest / len(cuts))
        loudness = loudness * jnp.repeat(jnp.exp(draws), shape[axis_at] // blocks).reshape((-1,) + (1,) * (len(shape) - 1 - axis_at))
    return loudness


def bell_draw(key, dims, deviation, bound, pieces=(), held_as=jnp.bfloat16):
    drawn = deviation * jax.random.normal(key, dims, jnp.float32)
    if pieces:
        drawn = drawn * block_scale(key, dims, pieces, -0.22, 0.18)
    return jnp.clip(drawn, -bound, bound).astype(held_as)


def setup_inputs(seed: int = 0) -> dict:
    key_of = jax.random.split(jax.random.key(seed), 8)
    return {
        "tokens": bell_draw(key_of[0], (TOKENS, D), 1.0, 6.0, ((0, 256),)),
        "weight": bell_draw(key_of[1], (D, QW), D ** -0.5, 0.078125, ((0, 32),)),
        "norm_gain": jnp.clip(1.0 + 0.18 * jax.random.normal(key_of[2], (QW,), jnp.float32), 0.1, 1.9),
        "cotangent": bell_draw(key_of[3], (TOKENS, QW), 1.0, 6.0, ((0, 256),)),
        "subspace": bell_draw(key_of[4], (QW, RANK), QW ** -0.5, 0.125),
        "moment": bell_draw(key_of[5], (D, RANK), 1.0, 6.0, ((0, 32),), jnp.float32),
        "second": jnp.clip(jnp.exp(math.log(2.0) - 3.6888794 * jax.random.uniform(key_of[6], (D, RANK), jnp.float32) ** block_scale(key_of[6], (D, RANK), ((0, 32),), -0.2, 0.2)), 0.05, 2.0),
    }


def adam_step(grad_low, moment, second, subspace):
    moment_new = 0.9 * moment + 0.1 * grad_low
    second_new = 0.999 * second + 0.001 * grad_low * grad_low
    coefficients = (moment_new / (jnp.sqrt(second_new) + 1e-08)).astype(jnp.bfloat16)
    update = lax.dot_general(coefficients, subspace, (((1,), (1,)), ((), ())), preferred_element_type=jnp.float32)
    return (moment_new, second_new, update)

def reference(tokens, weight, norm_gain, cotangent, subspace, moment, second):
    queries = jnp.dot(tokens, weight, preferred_element_type=jnp.float32)
    root_mean = jnp.sqrt(lax.optimization_barrier(jnp.mean(queries * queries, axis=1, keepdims=True)) + 1e-06)
    normed = (norm_gain * queries / root_mean).astype(jnp.bfloat16)
    scaled = norm_gain * cotangent.astype(jnp.float32)
    inner_sum = lax.optimization_barrier(jnp.sum(scaled * queries, axis=1, keepdims=True))
    query_grad = (scaled / root_mean - queries * inner_sum / (QW * root_mean ** 3)).astype(jnp.bfloat16)
    in_grad = lax.dot_general(query_grad, weight, (((1,), (1,)), ((), ())), preferred_element_type=jnp.float32).astype(jnp.bfloat16)
    projected = jnp.dot(query_grad, subspace, preferred_element_type=jnp.float32).astype(jnp.bfloat16)
    token_blocks = tokens.reshape(N_DP, N_FSDP, TOK_DEV, D)
    proj_blocks = projected.reshape(N_DP, N_FSDP, TOK_DEV, RANK)

    def group_total(pair):

        def add_block(running, item):
            block_term = lax.dot_general(item[0], item[1], (((0,), (0,)), ((), ())), preferred_element_type=jnp.float32)
            rounded = lax.optimization_barrier(block_term.astype(jnp.bfloat16))
            return (running + rounded.astype(jnp.float32), None)
        running, _ = lax.scan(add_block, jnp.zeros((D, RANK), jnp.float32), pair)
        return running
    group_sums = lax.map(group_total, (token_blocks, proj_blocks))
    grad_low = lax.optimization_barrier(jnp.sum(group_sums, axis=0)) * (1.0 / math.sqrt(TOKENS))
    moment_new, second_new, update = adam_step(grad_low, moment, second, subspace)
    return (normed, in_grad, moment_new, second_new, update)
```

```python
import math

import jax
import jax.numpy as jnp
from jax import lax
from jax.sharding import Mesh
from jax.sharding import PartitionSpec as P

AXES = ("y", "zl", "zh", "x", "c")
NY, NZL, NZH, NX, NC = 4, 2, 4, 4, 2
BF16, F32 = jnp.bfloat16, jnp.float32


def send(a, move):
    pairs = []

    def number(y, z, x, c):
        return (((y * NZL + z % NZL) * NZH + z // NZL) * NX + x) * NC + c

    for y in range(NY):
        for z in range(NZL * NZH):
            for x in range(NX):
                for c in range(NC):
                    pairs.append((number(y, z, x, c), number(*move(y, z, x, c))))
    return lax.ppermute(a, AXES, pairs)


def way(c):
    return 1 - 2 * c


def to_x(k):
    return lambda y, z, x, c: (y, z, (x + k * way(c)) % NX, c)


def to_y(k):
    return lambda y, z, x, c: ((y + k * way(c)) % NY, z, x, c)


def to_z(k):
    return lambda y, z, x, c: (y, (z + 2 * k * way(c)) % 8, x, c)


def to_core(y, z, x, c):
    return (y, z, x, 1 - c)


def to_home(y, z, x, c):
    return (y, (z - 2 * y * way(c)) % 8, x, c)


def to_z_pair(y, z, x, c):
    return (y, z ^ 1, x, c)


def pick(a, i, axis=0):
    return lax.dynamic_index_in_dim(a, i, axis, keepdims=False)


def around(a, at, sign, axis):
    return jnp.stack([pick(a, (at - r * sign) % 4, axis) for r in range(4)], axis)


def total(parts, dtype=BF16):
    out = parts[0].astype(F32)
    for part in parts[1:]:
        out = out + part.astype(F32)
    return out.astype(dtype)


def gather_weight(weight, y, sign):
    rows, width = weight.shape
    quarter, half = width // NY, rows // 2
    own = lax.dynamic_slice(weight, (0, y * quarter), (rows, quarter))
    by_z = {0: own}
    for k in (1, 3, 2):
        by_z[k] = send(own, to_z(k))
    first, second = {}, {}
    for batch in ((0,), (1, 3), (2,)):
        n = len(batch)
        high = jnp.stack([by_z[k][:half] for k in batch])
        low = jnp.stack([by_z[k][half:] for k in batch])
        if batch == (0,):
            strip = around(weight[half:].reshape(half, NY, quarter), y, sign, 1)
            strip = strip.reshape(1, half, width)
        else:
            strip = jnp.concatenate([low] + [send(low, to_y(r)) for r in (1, 2, 3)], axis=2)
        block = jnp.stack([high] + [send(high, to_x(r)) for r in (1, 2, 3)])
        blocks, strips = [block], [strip]
        for _ in range(3):
            strips.append(send(strips[-1], to_x(1)))
            blocks.append(send(blocks[-1], to_y(1)))
        whole = jnp.concatenate(blocks, axis=3)
        for i, k in enumerate(batch):
            first[k] = whole[:, i]
            second[k] = jnp.stack([s[i] for s in strips])
    return jnp.stack(
        [
            jnp.stack([first[k] for k in range(4)], axis=1),
            jnp.stack([second[k] for k in range(4)], axis=1),
        ]
    )


def local(tokens, weight, norm_gain, cotangent, subspace, moment, second):
    y, zh = lax.axis_index("y"), lax.axis_index("zh")
    x, c = lax.axis_index("x"), lax.axis_index("c")
    sign = 1 - 2 * c
    tok, depth = tokens.shape
    rows, width = weight.shape
    quarter = width // NY
    rank = subspace.shape[1]

    by_row = tokens.T.reshape(NZH * NX, NC, rows, tok)
    mine = pick(by_row, c, 1)
    other = send(pick(by_row, 1 - c, 1), to_core)
    pair = jnp.concatenate([mine, other], axis=2).reshape(NZH, NX, rows, 2 * tok)
    pair = around(around(pair, zh, sign, 0), x, sign, 1)
    pair_halves = pair.reshape(NZH, NX, 2, rows // 2, 2 * tok).transpose(2, 1, 0, 3, 4)
    pair_halves = pair_halves.reshape(depth // NC, 2 * tok)

    gain = around(norm_gain.reshape(NY, quarter), y, sign, 0).reshape(width)
    scaled = around(cotangent.reshape(tok, NY, quarter), y, sign, 1).reshape(tok, width)
    scaled = gain * scaled.astype(F32)
    basis = around(subspace.reshape(NY, quarter, rank), y, sign, 0).reshape(width, rank)

    matrix = gather_weight(weight, y, sign).reshape(depth // NC, width)
    partial = lax.dot_general(
        pair_halves, matrix, (((0,), (0,)), ((), ())), preferred_element_type=F32
    )
    swap = (0, 3, 2, 1)

    def swapped(a):
        return jnp.concatenate([a[:, r * quarter : (r + 1) * quarter] for r in swap], axis=1)

    queries = partial[:tok] + send(swapped(partial[tok:]), to_core)
    root_mean = jnp.sqrt(jnp.mean(queries * queries, axis=1, keepdims=True) + 1e-06)
    normed = (gain * queries / root_mean).astype(BF16)
    inner_sum = jnp.sum(scaled * queries, axis=1, keepdims=True)
    query_grad = (
        scaled / root_mean - queries * inner_sum / (width * root_mean**3)
    ).astype(BF16)
    projected = jnp.dot(query_grad, basis, preferred_element_type=F32).astype(BF16)
    both = jnp.concatenate([projected, send(projected, to_core)], axis=0)
    term = jnp.dot(
        pair.reshape(depth // NC, 2 * tok), both, preferred_element_type=F32
    ).astype(BF16)
    term = term.reshape(NZH, NX, rows, rank)
    left, right = term[..., : rank // 2], term[..., rank // 2 :]

    left = total([left[:, 0]] + [send(left[:, r], to_x(-r)) for r in (1, 2, 3)])
    right = total(
        [pick(right, y)]
        + [send(pick(right, (y - r * sign) % 4), to_y(-r)) for r in (1, 2, 3)]
    )
    left = total(
        [pick(left, y)] + [send(pick(left, (y - r * sign) % 4), to_y(-r)) for r in (1, 2, 3)]
    )
    right = total([right[0]] + [send(right[r], to_x(-r)) for r in (1, 2, 3)])
    mixed = send(jnp.concatenate([left, right], axis=1), to_home)
    mixed = total([mixed, send(mixed, to_z_pair)])
    parts = jnp.stack([mixed] + [send(mixed, to_y(r)) for r in (1, 2, 3)])
    ordered = [pick(parts, ((y - at) * sign) % 4) for at in range(4)]
    scale = 1.0 / math.sqrt(tok * NY * NZL * NZH * NX * NC)
    grad_low = total(ordered, F32) * scale

    moment_new = 0.9 * moment + 0.1 * grad_low
    second_new = 0.999 * second + 0.001 * grad_low * grad_low
    coefficients = (moment_new / (jnp.sqrt(second_new) + 1e-08)).astype(BF16)
    update = lax.dot_general(
        coefficients, subspace, (((1,), (1,)), ((), ())), preferred_element_type=F32
    )

    both_grad = jnp.concatenate([query_grad, send(swapped(query_grad), to_core)], axis=0)
    in_rows = lax.dot_general(
        matrix, both_grad, (((1,), (1,)), ((), ())), preferred_element_type=F32
    ).astype(BF16)
    in_rows = in_rows.reshape(2, NX, NZH, rows // 2, 2 * tok)
    came = send(in_rows[..., tok:], to_core)

    def absolute(a, s):
        a = a.transpose(2, 1, 0, 3, 4)
        a = jnp.stack([pick(a, ((zh - at) * s) % 4, 0) for at in range(4)], 0)
        a = jnp.stack([pick(a, ((x - at) * s) % 4, 1) for at in range(4)], 1)
        return a.reshape(NZH, NX, rows, tok)

    cores = jnp.stack([absolute(in_rows[..., :tok], sign), absolute(came, -sign)], axis=2)
    cores = jnp.stack([pick(cores, c, 2), pick(cores, 1 - c, 2)], axis=2)
    in_grad = cores.reshape(depth, tok).T
    normed = normed.reshape(tok, NY, quarter)
    normed = jnp.stack([pick(normed, ((y - at) * sign) % 4, 1) for at in range(4)], 1)
    return (normed.reshape(tok, width), in_grad, moment_new, second_new, update)


def solution(mesh):
    fine = Mesh(mesh.devices.reshape(NY, NZL, NZH, NX, NC), AXES)
    tokens_spec = P(("y", "zl", "zh", "x", "c"), None)
    rows_spec = P(("zh", "x", "c"), None)
    return jax.shard_map(
        local,
        mesh=fine,
        in_specs=(tokens_spec, rows_spec, P(), tokens_spec, P(), rows_spec, rows_spec),
        out_specs=(tokens_spec, tokens_spec, rows_spec, rows_spec, rows_spec),
        check_vma=False,
    )
```

```python
import math

import jax
import jax.numpy as jnp
from jax import lax
from jax.sharding import Mesh
from jax.sharding import PartitionSpec as P

AXES = ("y", "zl", "zh", "x", "c")
NY, NZL, NZH, NX, NC = 4, 2, 4, 4, 2
BF16, F32 = jnp.bfloat16, jnp.float32
SPLIT = 112


def send(a, move):
    pairs = []

    def number(y, z, x, c):
        return (((y * NZL + z % NZL) * NZH + z // NZL) * NX + x) * NC + c

    for y in range(NY):
        for z in range(NZL * NZH):
            for x in range(NX):
                for c in range(NC):
                    pairs.append((number(y, z, x, c), number(*move(y, z, x, c))))
    return lax.ppermute(a, AXES, pairs)


def way(c):
    return 1 - 2 * c


def to_x(k):
    return lambda y, z, x, c: (y, z, (x + k * way(c)) % NX, c)


def to_y(k):
    return lambda y, z, x, c: ((y + k * way(c)) % NY, z, x, c)


def to_z(k):
    return lambda y, z, x, c: (y, (z + 2 * k * way(c)) % 8, x, c)


def to_core(y, z, x, c):
    return (y, z, x, 1 - c)


def to_home(y, z, x, c):
    return (y, (z - 2 * y * way(c)) % 8, x, c)


def to_z_pair(y, z, x, c):
    return (y, z ^ 1, x, c)


def pick(a, i, axis=0):
    return lax.dynamic_index_in_dim(a, i, axis, keepdims=False)


def around(a, at, sign, axis):
    return jnp.stack([pick(a, (at - r * sign) % 4, axis) for r in range(4)], axis)


def total(parts, dtype=BF16):
    out = parts[0].astype(F32)
    for part in parts[1:]:
        out = out + part.astype(F32)
    return out.astype(dtype)


def after(a, *earlier):
    return lax.optimization_barrier((a, *earlier))[0]


def gather_weight(weight, y, sign):
    rows, width = weight.shape
    quarter = width // NY
    own = lax.dynamic_slice(weight, (0, y * quarter), (rows, quarter))
    by_z = [own] * NZH
    for k in (1, 3, 2):
        by_z[k] = send(own, to_z(k))
    level = around(weight.reshape(rows, NY, quarter), y, sign, 1).reshape(rows, width)
    level, *by_z[1:] = lax.optimization_barrier((level, *by_z[1:]))
    level = [level, send(level, to_x(1))]
    high = [jnp.stack([by_z[k][:SPLIT] for k in (1, 2, 3)])]
    low = [jnp.stack([by_z[k][SPLIT:] for k in (1, 2, 3)])]
    for _ in range(3):
        high.append(send(high[-1], to_x(1)))
        low.append(send(low[-1], to_y(1)))
    along = [after(jnp.concatenate(low, axis=2), high[-1])]
    for i in range(2):
        level.append(send(after(level[-1], high[-1], low[-1]), to_x(1)))
    for _ in range(3):
        along.append(send(along[-1], to_x(1)))
    across = []
    for i in (0, 2):
        block = [jnp.stack(high[i : i + 2])]
        for _ in range(3):
            block.append(send(block[-1], to_y(1)))
        across.append(block)
    across = [jnp.concatenate([across[0][r], across[1][r]]) for r in range(NY)]
    return level, across, along, (high[-1], low[-1])


def local(tokens, weight, norm_gain, cotangent, subspace, moment, second):
    y, zh = lax.axis_index("y"), lax.axis_index("zh")
    x, c = lax.axis_index("x"), lax.axis_index("c")
    sign = 1 - 2 * c
    tok, depth = tokens.shape
    rows, width = weight.shape
    quarter = width // NY
    rank = subspace.shape[1]

    level, across, along, begun = gather_weight(weight, y, sign)
    tokens, cotangent, subspace_here = lax.optimization_barrier(
        (tokens, cotangent, subspace, *begun)
    )[:3]

    by_row = tokens.T.reshape(NZH * NX, NC, rows, tok)
    mine = pick(by_row, c, 1)
    other = send(pick(by_row, 1 - c, 1), to_core)
    pair = jnp.concatenate([mine, other], axis=2).reshape(NZH, NX, rows, 2 * tok)
    pair = around(around(pair, zh, sign, 0), x, sign, 1)
    rest = pair[1:].transpose(1, 0, 2, 3)
    tok_level = pair[0].reshape(NX * rows, 2 * tok)
    tok_across = rest[:, :, :SPLIT].reshape(-1, 2 * tok)
    tok_along = rest[:, :, SPLIT:].reshape(-1, 2 * tok)

    gain = around(norm_gain.reshape(NY, quarter), y, sign, 0).reshape(width)
    scaled = around(cotangent.reshape(tok, NY, quarter), y, sign, 1).reshape(tok, width)
    scaled = gain * scaled.astype(F32)
    basis = around(subspace_here.reshape(NY, quarter, rank), y, sign, 0).reshape(width, rank)

    level = jnp.concatenate(level)
    across = [a.reshape(-1, quarter) for a in across]
    along = [a.reshape(-1, width) for a in along]

    def by_tokens(rows_of_tokens, a):
        return lax.dot_general(
            rows_of_tokens, a, (((0,), (0,)), ((), ())), preferred_element_type=F32
        )

    early = jnp.concatenate(along[:3])
    partial = by_tokens(tok_level, level) + by_tokens(tok_along[: early.shape[0]], early)
    partial = partial + by_tokens(tok_along[early.shape[0] :], along[3])
    partial = partial + jnp.concatenate([by_tokens(tok_across, a) for a in across], axis=1)
    swap = (0, 3, 2, 1)

    def swapped(a):
        return jnp.concatenate([a[:, r * quarter : (r + 1) * quarter] for r in swap], axis=1)

    queries = partial[:tok] + send(swapped(partial[tok:]), to_core)
    root_mean = jnp.sqrt(jnp.mean(queries * queries, axis=1, keepdims=True) + 1e-06)
    normed = (gain * queries / root_mean).astype(BF16)
    inner_sum = jnp.sum(scaled * queries, axis=1, keepdims=True)
    query_grad = (
        scaled / root_mean - queries * inner_sum / (width * root_mean**3)
    ).astype(BF16)
    both_grad = jnp.concatenate([query_grad, send(swapped(query_grad), to_core)], axis=0)
    projected = jnp.dot(query_grad, basis, preferred_element_type=F32).astype(BF16)
    both = jnp.concatenate([projected, send(projected, to_core)], axis=0)
    both, both_grad = lax.optimization_barrier((both, both_grad))
    term = jnp.dot(
        pair.reshape(depth // NC, 2 * tok), both, preferred_element_type=F32
    ).astype(BF16)
    term = term.reshape(NZH, NX, rows, rank)
    matrix = jnp.concatenate([level, jnp.concatenate(across, axis=1)] + along)
    in_rows = lax.dot_general(
        matrix, both_grad, (((1,), (1,)), ((), ())), preferred_element_type=F32
    ).astype(BF16)
    left, right = term[..., : rank // 2], term[..., rank // 2 :]

    left = total([left[:, 0]] + [send(left[:, r], to_x(-r)) for r in (1, 2, 3)])
    right = total(
        [pick(right, y)]
        + [send(pick(right, (y - r * sign) % 4), to_y(-r)) for r in (1, 2, 3)]
    )
    left, right, in_rows, normed = lax.optimization_barrier((left, right, in_rows, normed))
    left = total(
        [pick(left, y)] + [send(pick(left, (y - r * sign) % 4), to_y(-r)) for r in (1, 2, 3)]
    )
    right = total([right[0]] + [send(right[r], to_x(-r)) for r in (1, 2, 3)])
    mixed = send(jnp.concatenate([left, right], axis=1), to_home)
    mixed = total([mixed, send(mixed, to_z_pair)])
    parts = jnp.stack([mixed] + [send(mixed, to_y(r)) for r in (1, 2, 3)])
    ordered = [pick(parts, ((y - at) * sign) % 4) for at in range(4)]
    scale = 1.0 / math.sqrt(tok * NY * NZL * NZH * NX * NC)
    grad_low = total(ordered, F32) * scale

    moment_new = 0.9 * moment + 0.1 * grad_low
    second_new = 0.999 * second + 0.001 * grad_low * grad_low
    coefficients = (moment_new / (jnp.sqrt(second_new) + 1e-08)).astype(BF16)
    update = lax.dot_general(
        coefficients, subspace, (((1,), (1,)), ((), ())), preferred_element_type=F32
    )

    n_level, n_across = NX * rows, NX * 3 * SPLIT
    in_level = in_rows[:n_level].reshape(1, NX, rows, 2 * tok)
    in_across = in_rows[n_level : n_level + n_across].reshape(NX, 3, SPLIT, 2 * tok)
    in_along = in_rows[n_level + n_across :].reshape(NX, 3, rows - SPLIT, 2 * tok)
    in_rest = jnp.concatenate([in_across, in_along], axis=2).transpose(1, 0, 2, 3)
    in_rows = jnp.concatenate([in_level, in_rest])
    came = send(in_rows[..., tok:], to_core)

    def absolute(a, s):
        a = jnp.stack([pick(a, ((zh - at) * s) % 4, 0) for at in range(4)], 0)
        return jnp.stack([pick(a, ((x - at) * s) % 4, 1) for at in range(4)], 1)

    cores = jnp.stack([absolute(in_rows[..., :tok], sign), absolute(came, -sign)], axis=2)
    cores = jnp.stack([pick(cores, c, 2), pick(cores, 1 - c, 2)], axis=2)
    in_grad = cores.reshape(depth, tok).T
    normed = normed.reshape(tok, NY, quarter)
    normed = jnp.stack([pick(normed, ((y - at) * sign) % 4, 1) for at in range(4)], 1)
    return (normed.reshape(tok, width), in_grad, moment_new, second_new, update)


def solution(mesh):
    fine = Mesh(mesh.devices.reshape(NY, NZL, NZH, NX, NC), AXES)
    tokens_spec = P(("y", "zl", "zh", "x", "c"), None)
    rows_spec = P(("zh", "x", "c"), None)
    return jax.shard_map(
        local,
        mesh=fine,
        in_specs=(tokens_spec, rows_spec, P(), tokens_spec, P(), rows_spec, rows_spec),
        out_specs=(tokens_spec, tokens_spec, rows_spec, rows_spec, rows_spec),
        check_vma=False,
    )
```

```python
import math

import jax
import jax.numpy as jnp
from jax import lax
from jax.experimental import pallas as pl
from jax.experimental.pallas import tpu as pltpu
from jax.sharding import Mesh
from jax.sharding import PartitionSpec as P

AXES = ("y", "zl", "zh", "x", "c")
NY, NZL, NZH, NX, NC = 4, 2, 4, 4, 2
BF16, F32 = jnp.bfloat16, jnp.float32
ROWS, SPLIT = 160, 112


def send(a, move):
    pairs = []

    def number(y, z, x, c):
        return (((y * NZL + z % NZL) * NZH + z // NZL) * NX + x) * NC + c

    for y in range(NY):
        for z in range(NZL * NZH):
            for x in range(NX):
                for c in range(NC):
                    pairs.append((number(y, z, x, c), number(*move(y, z, x, c))))
    return lax.ppermute(a, AXES, pairs)


def way(c):
    return 1 - 2 * c


def to_x(k):
    return lambda y, z, x, c: (y, z, (x + k * way(c)) % NX, c)


def to_y(k):
    return lambda y, z, x, c: ((y + k * way(c)) % NY, z, x, c)


def to_z(k):
    return lambda y, z, x, c: (y, (z + 2 * k * way(c)) % 8, x, c)


def to_core(y, z, x, c):
    return (y, z, x, 1 - c)


def to_home(y, z, x, c):
    return (y, (z - 2 * y * way(c)) % 8, x, c)


def to_z_pair(y, z, x, c):
    return (y, z ^ 1, x, c)


def pick(a, i, axis=0):
    return lax.dynamic_index_in_dim(a, i, axis, keepdims=False)


def local_kernel(kernel, out_shape, scalars, arrays):
    size = sum(a.size * a.dtype.itemsize for a in arrays)
    return pl.pallas_call(
        kernel,
        in_specs=[pl.BlockSpec(memory_space=pltpu.SMEM) for _ in scalars]
        + [pl.BlockSpec(memory_space=pltpu.VMEM) for _ in arrays],
        out_specs=jax.tree.map(lambda _: pl.BlockSpec(memory_space=pltpu.VMEM), out_shape),
        out_shape=out_shape,
        compiler_params=pltpu.CompilerParams(vmem_limit_bytes=12 << 20),
        cost_estimate=pl.CostEstimate(flops=0, bytes_accessed=2 * size, transcendentals=0),
    )(*scalars, *arrays)


def part(i, size):
    return pl.ds(pl.multiple_of(i * size, size), size)


def reorder(a, order, axis):
    n = order.shape[0]
    size = a.shape[axis] // n

    def kernel(order, a, out):
        for r in range(n):
            to = slice(r * size, (r + 1) * size)
            if axis == 0:
                out[to, :] = a[part(order[r], size), :]
            else:
                out[:, to] = a[:, part(order[r], size)]

    return local_kernel(kernel, jax.ShapeDtypeStruct(a.shape, a.dtype), [order], [a])


def scale_cotangent(gain, cotangent, order):
    n = order.shape[0]
    tok, width = cotangent.shape
    size = width // n

    def kernel(order, gain, cotangent, gain_out, out):
        for r in range(n):
            to, at = slice(r * size, (r + 1) * size), part(order[r], size)
            gain_out[:, to] = gain[:, at]
            out[:, to] = gain[:, at] * cotangent[:, at].astype(F32)

    shapes = [jax.ShapeDtypeStruct((1, width), F32), jax.ShapeDtypeStruct((tok, width), F32)]
    return local_kernel(kernel, shapes, [order], [gain.reshape(1, width), cotangent])


def join_tokens(by_row, other, mine_at, other_at):
    n, rows, tok = other.shape

    def kernel(mine_at, other_at, by_row, other, out):
        for i in range(n):
            out[i, :, :tok] = by_row[mine_at[i]]
            out[i, :, tok:] = other[other_at[i]]

    shape = jax.ShapeDtypeStruct((n, rows, 2 * tok), by_row.dtype)
    return local_kernel(kernel, shape, [mine_at, other_at], [by_row, other])


def place_columns(mine, came, core, high, low):
    rows, tok = mine.shape

    def kernel(core, high, low, mine, came, out):
        is_first = core[0] == 0
        for i in range(NZH * NX // 2):
            pieces = []
            for at in (2 * i, 2 * i + 1):
                blocks = []
                for k, source in enumerate((mine, came)):
                    top = source[pl.ds(pl.multiple_of(high[k, at], 16), SPLIT), :]
                    end = source[pl.ds(pl.multiple_of(low[k, at], 16), ROWS - SPLIT), :]
                    blocks.append(jnp.concatenate([top, end], axis=0))
                pieces.append(jnp.where(is_first, blocks[0], blocks[1]))
                pieces.append(jnp.where(is_first, blocks[1], blocks[0]))
            out[:, 4 * ROWS * i : 4 * ROWS * (i + 1)] = jnp.concatenate(pieces, axis=0).T

    shape = jax.ShapeDtypeStruct((tok, 2 * rows), mine.dtype)
    return local_kernel(kernel, shape, [core, high, low], [mine, came])


def total(parts, dtype=BF16):
    out = parts[0].astype(F32)
    for part in parts[1:]:
        out = out + part.astype(F32)
    return out.astype(dtype)


def after(a, *earlier):
    return lax.optimization_barrier((a, *earlier))[0]


def gather_weight(weight, level, y, ready):
    rows, width = weight.shape
    quarter = width // NY
    own = lax.dynamic_slice(weight, (0, y * quarter), (rows, quarter))
    by_z = [own] * NZH
    for k in (1, 3, 2):
        by_z[k] = send(own, to_z(k))
    level = [level, send(level, to_x(1))]
    by_z = [after(a, level[1], ready) for a in by_z]
    high = [jnp.stack([by_z[k][:SPLIT] for k in (1, 2, 3)])]
    low = [jnp.stack([by_z[k][SPLIT:] for k in (1, 2, 3)])]
    for _ in range(3):
        high.append(send(high[-1], to_x(1)))
        low.append(send(low[-1], to_y(1)))
    even, odd = [jnp.stack(high[:2])], [jnp.stack(high[2:])]
    along = [after(jnp.concatenate(low, axis=2), odd[0])]
    level[1] = after(level[1], odd[0])
    for _ in range(2):
        level.append(send(level[-1], to_x(1)))
    for _ in range(3):
        even.append(send(even[-1], to_y(1)))
        odd.append(send(odd[-1], to_y(1)))
        along.append(send(along[-1], to_x(1)))
    across, begun = (even, odd), even[1]
    across = [jnp.concatenate([across[0][r], across[1][r]]) for r in range(NY)]
    return level, across, along, begun


def local(tokens, weight, norm_gain, cotangent, subspace, moment, second):
    y, zh = lax.axis_index("y"), lax.axis_index("zh")
    x, c = lax.axis_index("x"), lax.axis_index("c")
    sign = 1 - 2 * c
    tok, depth = tokens.shape
    rows, width = weight.shape
    quarter = width // NY
    rank = subspace.shape[1]

    steps = jnp.arange(4, dtype=jnp.int32)
    columns = (y - steps * sign) % 4
    blocks = ((zh - steps[:, None] * sign) % 4 * NX + (x - steps * sign) % 4).reshape(-1)

    own_level = reorder(weight, columns, 1)
    by_row = after(tokens, own_level).T.reshape(NZH * NX, NC, rows, tok)
    theirs = pick(by_row, 1 - c, 1)
    other = send(theirs, to_core)
    level, across, along, begun = gather_weight(weight, own_level, y, theirs)

    other = after(other, begun)
    pair = join_tokens(by_row.reshape(-1, rows, tok), other, blocks * NC + c, blocks)
    pair = pair.reshape(NZH, NX, rows, 2 * tok)
    rest = pair[1:].transpose(1, 0, 2, 3)
    tok_level = pair[0].reshape(NX * rows, 2 * tok)
    tok_across = rest[:, :, :SPLIT].reshape(-1, 2 * tok)
    tok_along = rest[:, :, SPLIT:].reshape(-1, 2 * tok)

    gain, scaled = scale_cotangent(norm_gain, after(cotangent, own_level), columns)
    basis = reorder(after(subspace, own_level), columns, 0)
    level = jnp.concatenate(level)
    across = [a.reshape(-1, quarter) for a in across]
    along = [a.reshape(-1, width) for a in along]

    def by_tokens(rows_of_tokens, a):
        return lax.dot_general(
            rows_of_tokens, a, (((0,), (0,)), ((), ())), preferred_element_type=F32
        )

    first = jnp.concatenate(along[:3])
    partial = by_tokens(tok_level, level) + by_tokens(tok_along[: first.shape[0]], first)
    partial = partial + by_tokens(tok_along[first.shape[0] :], along[3])
    partial = partial + jnp.concatenate([by_tokens(tok_across, a) for a in across], axis=1)
    swap = (0, 3, 2, 1)

    def swapped(a):
        return jnp.concatenate([a[:, r * quarter : (r + 1) * quarter] for r in swap], axis=1)

    queries = partial[:tok] + send(swapped(partial[tok:]), to_core)
    root_mean = jnp.sqrt(jnp.mean(queries * queries, axis=1, keepdims=True) + 1e-06)
    normed = (gain * queries / root_mean).astype(BF16)
    inner_sum = jnp.sum(scaled * queries, axis=1, keepdims=True)
    query_grad = (
        scaled / root_mean - queries * inner_sum / (width * root_mean**3)
    ).astype(BF16)
    their_grad = send(swapped(query_grad), to_core)
    projected = jnp.dot(query_grad, basis, preferred_element_type=F32).astype(BF16)
    both = jnp.concatenate([projected, send(projected, to_core)], axis=0)
    both, their_grad = lax.optimization_barrier((both, their_grad))
    term = jnp.dot(
        pair.reshape(depth // NC, 2 * tok), both, preferred_element_type=F32
    ).astype(BF16)
    term = term.reshape(NZH, NX, rows, rank)
    matrix = jnp.concatenate([level, jnp.concatenate(across, axis=1)] + along)

    def in_rows(grad):
        return lax.dot_general(
            matrix, grad, (((1,), (1,)), ((), ())), preferred_element_type=F32
        ).astype(BF16)

    in_theirs = in_rows(their_grad)
    in_mine = in_rows(after(query_grad, in_theirs))
    left, right = term[..., : rank // 2], term[..., rank // 2 :]

    left = total([left[:, 0]] + [send(left[:, r], to_x(-r)) for r in (1, 2, 3)])
    right = total(
        [pick(right, y)]
        + [send(pick(right, (y - r * sign) % 4), to_y(-r)) for r in (1, 2, 3)]
    )
    normed = reorder(normed, (((y - steps) * sign) % 4).astype(jnp.int32), 1)
    left, right, in_theirs, in_mine, normed = lax.optimization_barrier(
        (left, right, in_theirs, in_mine, normed)
    )
    left = total(
        [pick(left, y)] + [send(pick(left, (y - r * sign) % 4), to_y(-r)) for r in (1, 2, 3)]
    )
    right = total([right[0]] + [send(right[r], to_x(-r)) for r in (1, 2, 3)])
    came = send(in_theirs, to_core)
    mixed = after(jnp.concatenate([left, right], axis=1), came)
    mixed = send(mixed, to_home)
    high, low = [], []
    for s in (sign, -sign):
        dz = ((zh - steps[:, None]) * s) % 4
        dx = ((x - steps) * s) % 4
        block = dx * 3 + dz - 1
        start = NX * rows + NX * 3 * SPLIT
        high.append(jnp.where(dz == 0, dx * rows, NX * rows + block * SPLIT).reshape(-1))
        low.append(
            jnp.where(dz == 0, dx * rows + SPLIT, start + block * (rows - SPLIT)).reshape(-1)
        )
    high, low = (jnp.stack(a).astype(jnp.int32) for a in (high, low))
    in_grad = place_columns(in_mine, came, c.reshape(1), high, low)
    mixed, in_grad = lax.optimization_barrier((mixed, in_grad))
    mixed = total([mixed, send(mixed, to_z_pair)])
    parts = jnp.stack([mixed] + [send(mixed, to_y(r)) for r in (1, 2, 3)])
    ordered = [pick(parts, ((y - at) * sign) % 4) for at in range(4)]
    scale = 1.0 / math.sqrt(tok * NY * NZL * NZH * NX * NC)
    grad_low = total(ordered, F32) * scale

    moment_new = 0.9 * moment + 0.1 * grad_low
    second_new = 0.999 * second + 0.001 * grad_low * grad_low
    coefficients = (moment_new / (jnp.sqrt(second_new) + 1e-08)).astype(BF16)
    update = lax.dot_general(
        coefficients, subspace, (((1,), (1,)), ((), ())), preferred_element_type=F32
    )

    return (normed, in_grad, moment_new, second_new, update)


def solution(mesh):
    fine = Mesh(mesh.devices.reshape(NY, NZL, NZH, NX, NC), AXES)
    tokens_spec = P(("y", "zl", "zh", "x", "c"), None)
    rows_spec = P(("zh", "x", "c"), None)
    return jax.shard_map(
        local,
        mesh=fine,
        in_specs=(tokens_spec, rows_spec, P(), tokens_spec, P(), rows_spec, rows_spec),
        out_specs=(tokens_spec, tokens_spec, rows_spec, rows_spec, rows_spec),
        check_vma=False,
    )
```

```python
import math

import jax
import jax.numpy as jnp
from jax import lax
from jax.experimental import pallas as pl
from jax.experimental.pallas import tpu as pltpu
from jax.sharding import Mesh
from jax.sharding import PartitionSpec as P

AXES = ("y", "zl", "zh", "x", "c")
NY, NZL, NZH, NX, NC = 4, 2, 4, 4, 2
BF16, F32 = jnp.bfloat16, jnp.float32
ROWS, SPLIT = 160, 96


def send(a, move):
    pairs = []

    def number(y, z, x, c):
        return (((y * NZL + z % NZL) * NZH + z // NZL) * NX + x) * NC + c

    for y in range(NY):
        for z in range(NZL * NZH):
            for x in range(NX):
                for c in range(NC):
                    pairs.append((number(y, z, x, c), number(*move(y, z, x, c))))
    return lax.ppermute(a, AXES, pairs)


def way(c):
    return 1 - 2 * c


def to_x(k):
    return lambda y, z, x, c: (y, z, (x + k * way(c)) % NX, c)


def to_y(k):
    return lambda y, z, x, c: ((y + k * way(c)) % NY, z, x, c)


def to_z(k):
    return lambda y, z, x, c: (y, (z + 2 * k * way(c)) % 8, x, c)


def to_core(y, z, x, c):
    return (y, z, x, 1 - c)


def to_home(y, z, x, c):
    return (y, (z - 2 * y * way(c)) % 8, x, c)


def to_z_pair(y, z, x, c):
    return (y, z ^ 1, x, c)


def pick(a, i, axis=0):
    return lax.dynamic_index_in_dim(a, i, axis, keepdims=False)


def local_kernel(kernel, out_shape, scalars, arrays):
    size = sum(a.size * a.dtype.itemsize for a in arrays)
    return pl.pallas_call(
        kernel,
        in_specs=[pl.BlockSpec(memory_space=pltpu.SMEM) for _ in scalars]
        + [pl.BlockSpec(memory_space=pltpu.VMEM) for _ in arrays],
        out_specs=jax.tree.map(lambda _: pl.BlockSpec(memory_space=pltpu.VMEM), out_shape),
        out_shape=out_shape,
        compiler_params=pltpu.CompilerParams(vmem_limit_bytes=12 << 20),
        cost_estimate=pl.CostEstimate(flops=0, bytes_accessed=2 * size, transcendentals=0),
    )(*scalars, *arrays)


def part(i, size):
    return pl.ds(pl.multiple_of(i * size, size), size)


def reorder(a, order, axis):
    n = order.shape[0]
    size = a.shape[axis] // n

    def kernel(order, a, out):
        for r in range(n):
            to = slice(r * size, (r + 1) * size)
            if axis == 0:
                out[to, :] = a[part(order[r], size), :]
            else:
                out[:, to] = a[:, part(order[r], size)]

    return local_kernel(kernel, jax.ShapeDtypeStruct(a.shape, a.dtype), [order], [a])


def scale_cotangent(gain, cotangent, order):
    n = order.shape[0]
    tok, width = cotangent.shape
    size = width // n

    def kernel(order, gain, cotangent, gain_out, out):
        for r in range(n):
            to, at = slice(r * size, (r + 1) * size), part(order[r], size)
            gain_out[:, to] = gain[:, at]
            out[:, to] = gain[:, at] * cotangent[:, at].astype(F32)

    shapes = [jax.ShapeDtypeStruct((1, width), F32), jax.ShapeDtypeStruct((tok, width), F32)]
    return local_kernel(kernel, shapes, [order], [gain.reshape(1, width), cotangent])


def join_tokens(by_row, other, mine_at, other_at):
    n, rows, tok = other.shape

    def kernel(mine_at, other_at, by_row, other, out):
        for i in range(n):
            out[i, :, :tok] = by_row[mine_at[i]]
            out[i, :, tok:] = other[other_at[i]]

    shape = jax.ShapeDtypeStruct((n, rows, 2 * tok), by_row.dtype)
    return local_kernel(kernel, shape, [mine_at, other_at], [by_row, other])


def place_columns(mine, came, core, high, low):
    rows, tok = mine.shape

    def kernel(core, high, low, mine, came, out):
        is_first = core[0] == 0
        for i in range(NZH * NX // 2):
            pieces = []
            for at in (2 * i, 2 * i + 1):
                blocks = []
                for k, source in enumerate((mine, came)):
                    top = source[pl.ds(pl.multiple_of(high[k, at], 16), SPLIT), :]
                    end = source[pl.ds(pl.multiple_of(low[k, at], 16), ROWS - SPLIT), :]
                    blocks.append(jnp.concatenate([top, end], axis=0))
                pieces.append(jnp.where(is_first, blocks[0], blocks[1]))
                pieces.append(jnp.where(is_first, blocks[1], blocks[0]))
            out[:, 4 * ROWS * i : 4 * ROWS * (i + 1)] = jnp.concatenate(pieces, axis=0).T

    shape = jax.ShapeDtypeStruct((tok, 2 * rows), mine.dtype)
    return local_kernel(kernel, shape, [core, high, low], [mine, came])


def total(parts, dtype=BF16):
    out = parts[0].astype(F32)
    for part in parts[1:]:
        out = out + part.astype(F32)
    return out.astype(dtype)


def after(a, *earlier):
    return lax.optimization_barrier((a, *earlier))[0]


def gather_weight(weight, level, y, ready):
    rows, width = weight.shape
    quarter = width // NY
    own = lax.dynamic_slice(weight, (0, y * quarter), (rows, quarter))
    by_z = [own] * NZH
    for k in (1, 3, 2):
        by_z[k] = send(own, to_z(k))
    level = [level, send(level, to_x(1))]
    by_z = [after(a, level[1], ready) for a in by_z]
    high = [jnp.stack([by_z[k][:SPLIT] for k in (1, 2, 3)])]
    low = [jnp.stack([by_z[k][SPLIT:] for k in (1, 2, 3)])]
    for _ in range(3):
        high.append(send(high[-1], to_x(1)))
        low.append(send(low[-1], to_y(1)))
    even, odd = [jnp.stack(high[:2])], [jnp.stack(high[2:])]
    along = [after(jnp.concatenate(low, axis=2), odd[0])]
    level.append(send(level[1], to_x(1)))
    level.append(send(after(level[2], odd[0]), to_x(1)))
    for _ in range(3):
        even.append(send(even[-1], to_y(1)))
        odd.append(send(odd[-1], to_y(1)))
        along.append(send(along[-1], to_x(1)))
    across, begun, late = (even, odd), even[1], (odd[1], even[2])
    across = [jnp.concatenate([across[0][r], across[1][r]]) for r in range(NY)]
    return level, across, along, begun, late


def local(tokens, weight, norm_gain, cotangent, subspace, moment, second):
    y, zh = lax.axis_index("y"), lax.axis_index("zh")
    x, c = lax.axis_index("x"), lax.axis_index("c")
    sign = 1 - 2 * c
    tok, depth = tokens.shape
    rows, width = weight.shape
    quarter = width // NY
    rank = subspace.shape[1]

    steps = jnp.arange(4, dtype=jnp.int32)
    columns = (y - steps * sign) % 4
    blocks = ((zh - steps[:, None] * sign) % 4 * NX + (x - steps * sign) % 4).reshape(-1)

    own_level = reorder(weight, columns, 1)
    by_row = after(tokens, own_level).T.reshape(NZH * NX, NC, rows, tok)
    theirs = pick(by_row, 1 - c, 1)
    other = send(theirs, to_core)
    level, across, along, begun, late = gather_weight(weight, own_level, y, theirs)

    other = after(other, begun)
    pair = join_tokens(by_row.reshape(-1, rows, tok), other, blocks * NC + c, blocks)
    pair = pair.reshape(NZH, NX, rows, 2 * tok)
    rest = pair[1:].transpose(1, 0, 2, 3)
    tok_level = pair[0].reshape(NX * rows, 2 * tok)
    tok_across = rest[:, :, :SPLIT].reshape(-1, 2 * tok)
    tok_along = rest[:, :, SPLIT:].reshape(-1, 2 * tok)

    gain, scaled = scale_cotangent(norm_gain, after(cotangent, *late), columns)
    basis = reorder(after(subspace, *late), columns, 0)
    level = jnp.concatenate(level)
    across = [a.reshape(-1, quarter) for a in across]
    along = [a.reshape(-1, width) for a in along]

    def by_tokens(rows_of_tokens, a):
        return lax.dot_general(
            rows_of_tokens, a, (((0,), (0,)), ((), ())), preferred_element_type=F32
        )

    first = jnp.concatenate(along[:3])
    partial = by_tokens(tok_level, level) + by_tokens(tok_along[: first.shape[0]], first)
    partial = partial + by_tokens(tok_along[first.shape[0] :], along[3])
    partial = partial + jnp.concatenate([by_tokens(tok_across, a) for a in across], axis=1)
    swap = (0, 3, 2, 1)

    def swapped(a):
        return jnp.concatenate([a[:, r * quarter : (r + 1) * quarter] for r in swap], axis=1)

    queries = partial[:tok] + send(swapped(partial[tok:]), to_core)
    root_mean = jnp.sqrt(jnp.mean(queries * queries, axis=1, keepdims=True) + 1e-06)
    normed = (gain * queries / root_mean).astype(BF16)
    inner_sum = jnp.sum(scaled * queries, axis=1, keepdims=True)
    query_grad = (
        scaled / root_mean - queries * inner_sum / (width * root_mean**3)
    ).astype(BF16)
    their_grad = send(swapped(query_grad), to_core)
    projected = jnp.dot(query_grad, basis, preferred_element_type=F32).astype(BF16)
    both = jnp.concatenate([projected, send(projected, to_core)], axis=0)
    both, their_grad = lax.optimization_barrier((both, their_grad))
    term = jnp.dot(
        pair.reshape(depth // NC, 2 * tok), both, preferred_element_type=F32
    ).astype(BF16)
    term = term.reshape(NZH, NX, rows, rank)
    matrix = jnp.concatenate([level, jnp.concatenate(across, axis=1)] + along)

    def in_rows(grad):
        return lax.dot_general(
            matrix, grad, (((1,), (1,)), ((), ())), preferred_element_type=F32
        ).astype(BF16)

    in_theirs = in_rows(their_grad)
    in_mine = in_rows(after(query_grad, in_theirs))
    left, right = term[..., : rank // 2], term[..., rank // 2 :]

    left = total([left[:, 0]] + [send(left[:, r], to_x(-r)) for r in (1, 2, 3)])
    right = total(
        [pick(right, y)]
        + [send(pick(right, (y - r * sign) % 4), to_y(-r)) for r in (1, 2, 3)]
    )
    normed = reorder(normed, (((y - steps) * sign) % 4).astype(jnp.int32), 1)
    left, right, in_theirs, in_mine, normed = lax.optimization_barrier(
        (left, right, in_theirs, in_mine, normed)
    )
    left = total(
        [pick(left, y)] + [send(pick(left, (y - r * sign) % 4), to_y(-r)) for r in (1, 2, 3)]
    )
    right = total([right[0]] + [send(right[r], to_x(-r)) for r in (1, 2, 3)])
    came = send(in_theirs, to_core)
    mixed = after(jnp.concatenate([left, right], axis=1), came)
    mixed = send(mixed, to_home)
    high, low = [], []
    for s in (sign, -sign):
        dz = ((zh - steps[:, None]) * s) % 4
        dx = ((x - steps) * s) % 4
        block = dx * 3 + dz - 1
        start = NX * rows + NX * 3 * SPLIT
        high.append(jnp.where(dz == 0, dx * rows, NX * rows + block * SPLIT).reshape(-1))
        low.append(
            jnp.where(dz == 0, dx * rows + SPLIT, start + block * (rows - SPLIT)).reshape(-1)
        )
    high, low = (jnp.stack(a).astype(jnp.int32) for a in (high, low))
    in_grad = place_columns(in_mine, came, c.reshape(1), high, low)
    mixed, in_grad = lax.optimization_barrier((mixed, in_grad))
    mixed = total([mixed, send(mixed, to_z_pair)])
    parts = jnp.stack([mixed] + [send(mixed, to_y(r)) for r in (1, 2, 3)])
    ordered = [pick(parts, ((y - at) * sign) % 4) for at in range(4)]
    scale = 1.0 / math.sqrt(tok * NY * NZL * NZH * NX * NC)
    grad_low = total(ordered, F32) * scale

    moment_new = 0.9 * moment + 0.1 * grad_low
    second_new = 0.999 * second + 0.001 * grad_low * grad_low
    coefficients = (moment_new / (jnp.sqrt(second_new) + 1e-08)).astype(BF16)
    update = lax.dot_general(
        coefficients, subspace, (((1,), (1,)), ((), ())), preferred_element_type=F32
    )

    return (normed, in_grad, moment_new, second_new, update)


def solution(mesh):
    fine = Mesh(mesh.devices.reshape(NY, NZL, NZH, NX, NC), AXES)
    tokens_spec = P(("y", "zl", "zh", "x", "c"), None)
    rows_spec = P(("zh", "x", "c"), None)
    return jax.shard_map(
        local,
        mesh=fine,
        in_specs=(tokens_spec, rows_spec, P(), tokens_spec, P(), rows_spec, rows_spec),
        out_specs=(tokens_spec, tokens_spec, rows_spec, rows_spec, rows_spec),
        check_vma=False,
    )
```

```python
import math

import jax
import jax.numpy as jnp
from jax import lax
from jax.sharding import Mesh
from jax.sharding import PartitionSpec as P

AXES = ("y", "zl", "zh", "x", "c")
NY, NZL, NZH, NX, NC = 4, 2, 4, 4, 2
BF16, F32 = jnp.bfloat16, jnp.float32
SPLIT = 96


def send(a, move):
    pairs = []

    def number(y, z, x, c):
        return (((y * NZL + z % NZL) * NZH + z // NZL) * NX + x) * NC + c

    for y in range(NY):
        for z in range(NZL * NZH):
            for x in range(NX):
                for c in range(NC):
                    pairs.append((number(y, z, x, c), number(*move(y, z, x, c))))
    return lax.ppermute(a, AXES, pairs)


def way(c):
    return 1 - 2 * c


def to_x(k):
    return lambda y, z, x, c: (y, z, (x + k * way(c)) % NX, c)


def to_y(k):
    return lambda y, z, x, c: ((y + k * way(c)) % NY, z, x, c)


def to_z(k):
    return lambda y, z, x, c: (y, (z + 2 * k * way(c)) % 8, x, c)


def to_core(y, z, x, c):
    return (y, z, x, 1 - c)


def to_home(y, z, x, c):
    return (y, (z - 2 * y * way(c)) % 8, x, c)


def to_z_pair(y, z, x, c):
    return (y, z ^ 1, x, c)


def pick(a, i, axis=0):
    return lax.dynamic_index_in_dim(a, i, axis, keepdims=False)


def around(a, at, sign, axis):
    return jnp.stack([pick(a, (at - r * sign) % 4, axis) for r in range(4)], axis)


def total(parts, dtype=BF16):
    out = parts[0].astype(F32)
    for part in parts[1:]:
        out = out + part.astype(F32)
    return out.astype(dtype)


def after(a, *earlier):
    return lax.optimization_barrier((a, *earlier))[0]


def gather_weight(weight, y, sign):
    rows, width = weight.shape
    quarter = width // NY
    own = lax.dynamic_slice(weight, (0, y * quarter), (rows, quarter))
    by_z = [own] * NZH
    for k in (1, 3, 2):
        by_z[k] = send(own, to_z(k))
    level = around(weight.reshape(rows, NY, quarter), y, sign, 1).reshape(rows, width)
    level, *by_z[1:] = lax.optimization_barrier((level, *by_z[1:]))
    level = [level, send(level, to_x(1))]
    high = [jnp.stack([by_z[k][:SPLIT] for k in (1, 2, 3)])]
    low = [jnp.stack([by_z[k][SPLIT:] for k in (1, 2, 3)])]
    for _ in range(3):
        high.append(send(high[-1], to_x(1)))
        low.append(send(low[-1], to_y(1)))
    along = [after(jnp.concatenate(low, axis=2), high[-1])]
    for i in range(2):
        level.append(send(after(level[-1], high[-1], low[-1]), to_x(1)))
    for _ in range(3):
        along.append(send(along[-1], to_x(1)))
    across = []
    for i in (0, 2):
        block = [jnp.stack(high[i : i + 2])]
        for _ in range(3):
            block.append(send(block[-1], to_y(1)))
        across.append(block)
    across = [jnp.concatenate([across[0][r], across[1][r]]) for r in range(NY)]
    return level, across, along, (high[-1], low[-1])


def local(tokens, weight, norm_gain, cotangent, subspace, moment, second):
    y, zh = lax.axis_index("y"), lax.axis_index("zh")
    x, c = lax.axis_index("x"), lax.axis_index("c")
    sign = 1 - 2 * c
    tok, depth = tokens.shape
    rows, width = weight.shape
    quarter = width // NY
    rank = subspace.shape[1]

    level, across, along, begun = gather_weight(weight, y, sign)
    tokens, cotangent, subspace_here = lax.optimization_barrier(
        (tokens, cotangent, subspace, *begun)
    )[:3]

    by_row = tokens.T.reshape(NZH * NX, NC, rows, tok)
    mine = pick(by_row, c, 1)
    other = send(pick(by_row, 1 - c, 1), to_core)
    pair = jnp.concatenate([mine, other], axis=2).reshape(NZH, NX, rows, 2 * tok)
    pair = around(around(pair, zh, sign, 0), x, sign, 1)
    rest = pair[1:].transpose(1, 0, 2, 3)
    tok_level = pair[0].reshape(NX * rows, 2 * tok)
    tok_across = rest[:, :, :SPLIT].reshape(-1, 2 * tok)
    tok_along = rest[:, :, SPLIT:].reshape(-1, 2 * tok)

    gain = around(norm_gain.reshape(NY, quarter), y, sign, 0).reshape(width)
    scaled = around(cotangent.reshape(tok, NY, quarter), y, sign, 1).reshape(tok, width)
    scaled = gain * scaled.astype(F32)
    basis = around(subspace_here.reshape(NY, quarter, rank), y, sign, 0).reshape(width, rank)

    level = jnp.concatenate(level)
    across = [a.reshape(-1, quarter) for a in across]
    along = [a.reshape(-1, width) for a in along]

    def by_tokens(rows_of_tokens, a):
        return lax.dot_general(
            rows_of_tokens, a, (((0,), (0,)), ((), ())), preferred_element_type=F32
        )

    early = jnp.concatenate(along[:3])
    partial = by_tokens(tok_level, level) + by_tokens(tok_along[: early.shape[0]], early)
    partial = partial + by_tokens(tok_along[early.shape[0] :], along[3])
    partial = partial + jnp.concatenate([by_tokens(tok_across, a) for a in across], axis=1)
    swap = (0, 3, 2, 1)

    def swapped(a):
        return jnp.concatenate([a[:, r * quarter : (r + 1) * quarter] for r in swap], axis=1)

    queries = partial[:tok] + send(swapped(partial[tok:]), to_core)
    root_mean = jnp.sqrt(jnp.mean(queries * queries, axis=1, keepdims=True) + 1e-06)
    normed = (gain * queries / root_mean).astype(BF16)
    inner_sum = jnp.sum(scaled * queries, axis=1, keepdims=True)
    query_grad = (
        scaled / root_mean - queries * inner_sum / (width * root_mean**3)
    ).astype(BF16)
    both_grad = jnp.concatenate([query_grad, send(swapped(query_grad), to_core)], axis=0)
    projected = jnp.dot(query_grad, basis, preferred_element_type=F32).astype(BF16)
    both = jnp.concatenate([projected, send(projected, to_core)], axis=0)
    both, both_grad = lax.optimization_barrier((both, both_grad))
    term = jnp.dot(
        pair.reshape(depth // NC, 2 * tok), both, preferred_element_type=F32
    ).astype(BF16)
    term = term.reshape(NZH, NX, rows, rank)
    matrix = jnp.concatenate([level, jnp.concatenate(across, axis=1)] + along)
    in_rows = lax.dot_general(
        matrix, both_grad, (((1,), (1,)), ((), ())), preferred_element_type=F32
    ).astype(BF16)
    left, right = term[..., : rank // 2], term[..., rank // 2 :]

    left = total([left[:, 0]] + [send(left[:, r], to_x(-r)) for r in (1, 2, 3)])
    right = total(
        [pick(right, y)]
        + [send(pick(right, (y - r * sign) % 4), to_y(-r)) for r in (1, 2, 3)]
    )
    left, right, in_rows, normed = lax.optimization_barrier((left, right, in_rows, normed))
    left = total(
        [pick(left, y)] + [send(pick(left, (y - r * sign) % 4), to_y(-r)) for r in (1, 2, 3)]
    )
    right = total([right[0]] + [send(right[r], to_x(-r)) for r in (1, 2, 3)])
    mixed = send(jnp.concatenate([left, right], axis=1), to_home)
    mixed = total([mixed, send(mixed, to_z_pair)])
    parts = jnp.stack([mixed] + [send(mixed, to_y(r)) for r in (1, 2, 3)])
    ordered = [pick(parts, ((y - at) * sign) % 4) for at in range(4)]
    scale = 1.0 / math.sqrt(tok * NY * NZL * NZH * NX * NC)
    grad_low = total(ordered, F32) * scale

    moment_new = 0.9 * moment + 0.1 * grad_low
    second_new = 0.999 * second + 0.001 * grad_low * grad_low
    coefficients = (moment_new / (jnp.sqrt(second_new) + 1e-08)).astype(BF16)
    update = lax.dot_general(
        coefficients, subspace, (((1,), (1,)), ((), ())), preferred_element_type=F32
    )

    n_level, n_across = NX * rows, NX * 3 * SPLIT
    in_level = in_rows[:n_level].reshape(1, NX, rows, 2 * tok)
    in_across = in_rows[n_level : n_level + n_across].reshape(NX, 3, SPLIT, 2 * tok)
    in_along = in_rows[n_level + n_across :].reshape(NX, 3, rows - SPLIT, 2 * tok)
    in_rest = jnp.concatenate([in_across, in_along], axis=2).transpose(1, 0, 2, 3)
    in_rows = jnp.concatenate([in_level, in_rest])
    came = send(in_rows[..., tok:], to_core)

    def absolute(a, s):
        a = jnp.stack([pick(a, ((zh - at) * s) % 4, 0) for at in range(4)], 0)
        return jnp.stack([pick(a, ((x - at) * s) % 4, 1) for at in range(4)], 1)

    cores = jnp.stack([absolute(in_rows[..., :tok], sign), absolute(came, -sign)], axis=2)
    cores = jnp.stack([pick(cores, c, 2), pick(cores, 1 - c, 2)], axis=2)
    in_grad = cores.reshape(depth, tok).T
    normed = normed.reshape(tok, NY, quarter)
    normed = jnp.stack([pick(normed, ((y - at) * sign) % 4, 1) for at in range(4)], 1)
    return (normed.reshape(tok, width), in_grad, moment_new, second_new, update)


def solution(mesh):
    fine = Mesh(mesh.devices.reshape(NY, NZL, NZH, NX, NC), AXES)
    tokens_spec = P(("y", "zl", "zh", "x", "c"), None)
    rows_spec = P(("zh", "x", "c"), None)
    return jax.shard_map(
        local,
        mesh=fine,
        in_specs=(tokens_spec, rows_spec, P(), tokens_spec, P(), rows_spec, rows_spec),
        out_specs=(tokens_spec, tokens_spec, rows_spec, rows_spec, rows_spec),
        check_vma=False,
    )
```
